256 devices in a mesh: pipe: 8 (over z), seq: 32 (over y, x, core).
Axes of the slice: x: 4, y: 4, z: 8, core: 2. Of those that a mesh axis runs over, the one named last changes fastest.
Arguments:
- section_input: bfloat16 [8, 8192, 1024], P('pipe', 'seq'), may hold values from -6 to 6
- saved_input: bfloat16 [8, 8192, 1024], P('pipe', 'seq'), may hold values from -6 to 6
- grad_output: bfloat16 [8, 8192, 1024], P('pipe', 'seq'), may hold values from -6 to 6
- w_qkv: bfloat16 [8, 3072, 1024], P('pipe'), may hold values from -0.1875 to 0.1875
- w_out: bfloat16 [8, 1024, 1024], P('pipe'), may hold values from -0.75 to 0.75
- tile_cluster: int32 [64], replicated, may hold values from 0 to 31, as said below
Outputs:
- next_input: bfloat16 [8, 8192, 1024], P('pipe', 'seq')
- grad_input: bfloat16 [8, 8192, 1024], P('pipe', 'seq')
The draws below stay inside these ranges and needn't reach their ends.
Inputs may be any that keep to these rules, and one draw needn't show every extreme that they name: `tile_cluster`: each of the 32 ids names between 1 and 3 tiles, and some id names exactly 3. The id of tile i leaves the remainder i % 4 when divided by 4.
All inputs are finite; a program needn't handle non-finite values.
Results may differ from the reference program's by a relative error of at most 0.007.
Values may be sent and summed in bfloat16 or wider, within the bound.
A program may use at most 128 MiB of HBM per device.

```python
import jax
import jax.numpy as jnp
from jax import lax

D = 1024
HEADS = 8
HD = 128
TILE = 128
INNER = 1024
TPD = 2
CAP = 3
TOKENS = 8192
NT = 64
CLUSTERS = 32
SECTIONS = 8


def shuffled_rows(key, count, length):
    keys = jax.random.split(key, count)
    rows = [jax.random.permutation(keys[index], length) for index in range(count)]
    return jnp.stack(rows).astype(jnp.int32)


def draw_tile_cluster(key, part):
    key_pattern, key_turn, key_order, key_label = jax.random.split(key, 4)
    spacing = CLUSTERS // HEADS
    members = TPD * HEADS
    pair_count = CLUSTERS // 2
    patterns = jnp.array([[TPD, TPD], [2 * TPD - 1, 1], [TPD + 1, TPD - 1]], dtype=jnp.int32)
    chosen = jax.random.randint(key_pattern, (pair_count,), 0, 3).at[0].set(1)
    turned = jax.random.randint(key_turn, (pair_count,), 0, 2)
    picked = patterns[chosen]
    columns = (jnp.arange(2)[None, :] + turned[:, None]) % 2
    cluster_size = jnp.take_along_axis(picked, columns, axis=1).reshape(spacing, HEADS)
    bounds = jnp.cumsum(cluster_size, axis=1)
    position = jnp.arange(members, dtype=jnp.int32)
    grouped = jnp.sum((position[None, :, None] >= bounds[:, None, :]).astype(jnp.int32), axis=2)
    orders = shuffled_rows(key_order, spacing, members)
    shuffled = jnp.take_along_axis(grouped, orders, axis=1)
    labels = shuffled_rows(key_label, spacing, HEADS)
    ranked = jnp.take_along_axis(labels, shuffled, axis=1)
    residue = jnp.arange(spacing, dtype=jnp.int32)[:, None]
    cluster = residue + spacing * ranked
    return cluster.T.reshape(NT).astype(jnp.int32)


def levels(key, dims, cuts, low, largest):
    level, own = 1.0, jax.random.fold_in(key, 6)
    for dim, shards_of in cuts:
        steps = jnp.exp(jax.random.uniform(jax.random.fold_in(own, dim), (shards_of,), jnp.float32, low / len(cuts), largest / len(cuts)))
        level = level * jnp.repeat(steps, dims[dim] // shards_of).reshape([-1 if axis == dim else 1 for axis in range(len(dims))])
    return level


def scatter_about(stream_key, shape, deviation, bound, cuts=(), held_as=jnp.bfloat16):
    result = jax.random.normal(stream_key, shape, jnp.float32) * deviation
    if len(cuts) > 0:
        result = levels(stream_key, shape, cuts, -0.22, 0.18) * result
    return jnp.clip(result, min=-bound, max=bound).astype(held_as)


def setup_inputs(seed: int = 0) -> dict:
    seeds = jax.random.split(jax.random.key(seed), 7)
    return {
        "section_input": scatter_about(seeds[0], (SECTIONS, TOKENS, D), 1.0, 6.0, ((0, 8), (1, 32))),
        "saved_input": scatter_about(seeds[1], (SECTIONS, TOKENS, D), 1.0, 6.0, ((0, 8), (1, 32))),
        "grad_output": scatter_about(seeds[2], (SECTIONS, TOKENS, D), 1.0, 6.0, ((0, 8), (1, 32))),
        "w_qkv": scatter_about(seeds[3], (SECTIONS, 3 * INNER, D), D ** -0.5, 0.1875, ((0, 8),)),
        "w_out": scatter_about(seeds[4], (SECTIONS, INNER, D), (INNER // 16) ** -0.5, 0.75, ((0, 8),)),
        "tile_cluster": draw_tile_cluster(jax.random.fold_in(seeds[6], 71), 0),
    }


EPSILON = 1e-05

def row_norm(values):
    return values * lax.rsqrt(lax.optimization_barrier(jnp.mean(values * values, axis=-1, keepdims=True)) + EPSILON)

def head_norm(values):
    shaped = values.reshape(values.shape[:-1] + (HEADS, HD))
    return row_norm(shaped).reshape(values.shape)

def attend(queries, key_rows, value_rows, live_keys):
    factor = queries.shape[-1] ** (-0.5)
    scores = jnp.dot(queries, key_rows.T, preferred_element_type=jnp.float32) * factor
    weights = jnp.where(live_keys[None, :], jnp.exp(scores), 0.0)
    softmax = weights / lax.optimization_barrier(jnp.sum(weights, axis=1, keepdims=True))
    soft_low = softmax.astype(jnp.bfloat16)
    return (softmax, soft_low, jnp.dot(soft_low, value_rows, preferred_element_type=jnp.float32))

def attend_forward(queries, key_rows, value_rows, live_keys):
    return (attend(queries, key_rows, value_rows, live_keys)[2],)

def attend_back(queries, key_rows, value_rows, grad_rows, live_keys):
    factor = queries.shape[-1] ** (-0.5)
    softmax, soft_low, outputs = attend(queries, key_rows, value_rows, live_keys)
    row_delta = lax.optimization_barrier(jnp.sum(grad_rows.astype(jnp.float32) * outputs, axis=1, keepdims=True))
    grad_soft = jnp.dot(grad_rows, value_rows.T, preferred_element_type=jnp.float32)
    grad_scores = (softmax * (grad_soft - row_delta)).astype(jnp.bfloat16)
    grad_queries = jnp.dot(grad_scores, key_rows, preferred_element_type=jnp.float32) * factor
    grad_keys = jnp.dot(grad_scores.T, queries, preferred_element_type=jnp.float32) * factor
    grad_values = jnp.dot(soft_low.T, grad_rows, preferred_element_type=jnp.float32)
    return (grad_queries, grad_keys, grad_values)

def by_cluster(tile_cluster, tensors, step, result_count):
    tile_ids = jnp.arange(NT, dtype=jnp.int32)
    lanes = jnp.arange(TILE, dtype=jnp.int32)
    slot_ids = jnp.arange(CAP, dtype=jnp.int32)
    in_axes = tuple((0 for tensor in tensors)) + (None,)

    def visit(totals, cluster):
        inside = tile_cluster == cluster
        members = jnp.argsort(jnp.where(inside, tile_ids, NT + tile_ids), stable=True)[:CAP].astype(jnp.int32)
        live_tiles = slot_ids < jnp.sum(inside.astype(jnp.int32))
        rows = (members[:, None] * TILE + lanes[None, :]).reshape(CAP * TILE)
        live_rows = jnp.repeat(live_tiles, TILE)
        pieces = []
        for tensor in tensors:
            picked = jnp.where(live_rows[:, None], tensor[rows], 0)
            pieces.append(picked.reshape(CAP * TILE, HEADS, HD).transpose(1, 0, 2))
        results = jax.vmap(step, in_axes=in_axes)(*pieces, live_rows)
        merged = tuple((total.at[rows].add(jnp.where(live_rows[:, None], part.transpose(1, 0, 2).reshape(CAP * TILE, INNER), 0.0)) for total, part in zip(totals, results)))
        return (merged, None)
    start = tuple((jnp.zeros((TOKENS, INNER), jnp.float32) for index in range(result_count)))
    totals, unused = lax.scan(visit, start, jnp.arange(CLUSTERS, dtype=jnp.int32))
    return totals

def split_heads(mixed):
    queries = head_norm(mixed[:, :INNER]).astype(jnp.bfloat16)
    key_rows = head_norm(mixed[:, INNER:2 * INNER]).astype(jnp.bfloat16)
    value_rows = mixed[:, 2 * INNER:].astype(jnp.bfloat16)
    return (queries, key_rows, value_rows)

def project(current, w_mix):
    normed = row_norm(current.astype(jnp.float32)).astype(jnp.bfloat16)
    return jnp.dot(normed, w_mix.T, preferred_element_type=jnp.float32)

def forward_section(current, w_mix, w_fin, tile_cluster):
    mixed = project(current, w_mix)
    queries, key_rows, value_rows = split_heads(mixed)
    totals = by_cluster(tile_cluster, (queries, key_rows, value_rows), attend_forward, 1)
    attention = totals[0].astype(jnp.bfloat16)
    return (current.astype(jnp.float32) + jnp.dot(attention, w_fin, preferred_element_type=jnp.float32)).astype(jnp.bfloat16)

def backward_section(stored, upstream, w_mix, w_fin, tile_cluster):
    mixed = project(stored, w_mix)
    queries, key_rows, value_rows = split_heads(mixed)
    grad_attention = jnp.dot(upstream, w_fin.T, preferred_element_type=jnp.float32).astype(jnp.bfloat16)
    totals = by_cluster(tile_cluster, (queries, key_rows, value_rows, grad_attention), attend_back, 3)
    grad_queries = totals[0].astype(jnp.bfloat16)
    grad_keys = totals[1].astype(jnp.bfloat16)
    grad_values = totals[2].astype(jnp.bfloat16)
    unused, pull_query = jax.vjp(head_norm, mixed[:, :INNER])
    unused, pull_key = jax.vjp(head_norm, mixed[:, INNER:2 * INNER])
    grad_mixed = jnp.concatenate([pull_query(grad_queries.astype(jnp.float32))[0], pull_key(grad_keys.astype(jnp.float32))[0], grad_values.astype(jnp.float32)], axis=1).astype(jnp.bfloat16)
    grad_normed = jnp.dot(grad_mixed, w_mix, preferred_element_type=jnp.float32)
    unused, pull_norm = jax.vjp(row_norm, stored.astype(jnp.float32))
    grad_norm_in = pull_norm(grad_normed)[0]
    return (upstream.astype(jnp.float32) + grad_norm_in).astype(jnp.bfloat16)

def reference(section_input, saved_input, grad_output, w_qkv, w_out, tile_cluster):
    forward_outs = []
    backward_outs = []
    for section in range(SECTIONS):
        forward_outs.append(forward_section(section_input[section], w_qkv[section], w_out[section], tile_cluster))
        backward_outs.append(backward_section(saved_input[section], grad_output[section], w_qkv[section], w_out[section], tile_cluster))
    blank = jnp.zeros((TOKENS, D), jnp.bfloat16)
    next_input = jnp.stack([blank] + forward_outs[:-1])
    grad_input = jnp.stack(backward_outs[1:] + [blank])
    return (next_input, grad_input)
```

```python
import jax
import jax.numpy as jnp
from jax import lax
from jax.experimental import pallas as pl
from jax.experimental.pallas import tpu as pltpu
from jax.sharding import PartitionSpec as P

MESH = pl.DeviceIdType.MESH
HEADS = 8
HD = 128
TILE = 128
D = 1024
GROUP = 16
CAP = 3
LIST = 8
EPS = 1e-05
FACTOR = HD ** (-0.5)
F32 = jnp.float32
BF16 = jnp.bfloat16


def nt(a, b):
    return lax.dot_general(a, b, (((1,), (1,)), ((), ())), preferred_element_type=F32)


def tn(a, b):
    return lax.dot_general(a, b, (((0,), (0,)), ((), ())), preferred_element_type=F32)


def nn(a, b):
    return jnp.dot(a, b, preferred_element_type=F32)


def inv_rms(u):
    return lax.rsqrt(jnp.mean(u * u, axis=-1, keepdims=True) + EPS)


def ring_order(i):
    return (1 + 2 * i - 3 * (i // 2)) % 4


def landed(ref, sem):
    pltpu.make_async_copy(ref, ref, sem).wait()


def kernel(
    tc_ref, x_hbm, xs_hbm, g_hbm, wq_hbm, wo_hbm,
    on_hbm, og_hbm,
    wq, wo, xin, xn, mixed, sf, sb, rf, rb, dst, ptm, fo, fr, bo, br, att, gm, gn, res,
    lists,
    w_sem, ex_ss, ex_rs, f_ss, f_rs, b_ss, b_rs, d_ss, d_rs,
    fo_ss, fo_rs, dq_ss, dq_rs, dkv_ss, dkv_rs, pf_ss, pf_rs, pb_ss, pb_rs,
):
    z = lax.axis_index("pipe")
    s = lax.axis_index("seq")
    y = s // 8
    x = (s // 2) % 4
    c = s % 2

    def seq_of(xx, yy, cc):
        return (yy * 4 + xx) * 2 + cc

    def f_dev(h):
        return (z, seq_of(x, h // 2, h % 2))

    def b_dev(h):
        return (z, seq_of(h // 2, y, h % 2))

    f_me = y * 2 + c
    b_me = x * 2 + c
    up = (z + 1) % 8
    down = (z + 7) % 8

    w_copies = [
        pltpu.make_async_copy(wq_hbm.at[0], wq, w_sem.at[0]),
        pltpu.make_async_copy(wo_hbm.at[0], wo, w_sem.at[1]),
    ]
    for copy in w_copies:
        copy.start()

    barrier = pltpu.get_barrier_semaphore()

    def greet(dev):
        pl.semaphore_signal(barrier, inc=1, device_id=dev, device_id_type=MESH)

    for i in range(1, 8):
        greet(f_dev((f_me + i) % 8))
    for i in range(2, 8):
        greet(b_dev((2 * x + i) % 8))
    for k in range(2):
        for zz in (up, down):
            greet((zz, seq_of(2 * c + k, y, x // 2)))
            greet((zz, seq_of(x, 2 * c + k, y // 2)))
    pl.semaphore_wait(barrier, 21)

    def exchange(t, src_hbm, j, forward):
        other = 2 * c + j
        own = x if forward else y
        dev = (z, seq_of(other, y, x // 2) if forward else seq_of(x, other, y // 2))
        src = src_hbm.at[0, pl.ds(j * TILE, TILE)]
        dst_ref = xin.at[t, pl.ds((own % 2) * TILE, TILE)]
        recv = ex_rs.at[t, own % 2]

        @pl.when(own == other)
        def _():
            pltpu.make_async_copy(src, dst_ref, recv).start()

        @pl.when(own != other)
        def _():
            pltpu.make_async_remote_copy(
                src_ref=src, dst_ref=dst_ref, send_sem=ex_ss.at[t, j], recv_sem=recv,
                device_id=dev, device_id_type=MESH,
            ).start()

    def exchange_sent(t, j, forward):
        own = x if forward else y

        @pl.when(own != 2 * c + j)
        def _():
            landed(xin.at[t, pl.ds(j * TILE, TILE)], ex_ss.at[t, j])

    def exchange_wait(t):
        for k in range(2):
            landed(xin.at[t, pl.ds(k * TILE, TILE)], ex_rs.at[t, k])

    for j in range(2):
        exchange(1, xs_hbm, j, False)
        exchange(0, x_hbm, j, True)
    for j in range(2):
        exchange(2, g_hbm, j, False)

    def fill(base, tile_of):
        ids = [tc_ref[tile_of(q)] for q in range(GROUP)]

        def one(q, carry):
            own_id = tc_ref[tile_of(q)]
            count = jnp.int32(0)
            rank = jnp.int32(0)
            members = [jnp.int32(GROUP)] * CAP
            for p in range(GROUP):
                same = ids[p] == own_id
                members = [
                    jnp.where(same & (count == k), p, members[k]) for k in range(CAP)
                ]
                rank = rank + jnp.where(same & (p < q), 1, 0)
                count = count + jnp.where(same, 1, 0)
            row = base + q * LIST
            for k in range(CAP):
                lists[row + k] = members[k]
            lists[row + 3] = jnp.minimum(rank, CAP - 1)
            lists[row + 4] = count
            return carry

        lax.fori_loop(0, GROUP, one, 0)

    fill(0, lambda q: 4 * q + x)
    fill(GROUP * LIST, lambda q: 4 * ((q % 4) * 4 + q // 4) + y)

    zero = jnp.zeros((TILE, HD), BF16)
    for t in range(3):
        rf[t, GROUP] = zero
    for t in range(4):
        rb[t, GROUP] = zero
    for k in range(CAP):
        dst[GROUP, k] = zero
        ptm[GROUP, k] = zero

    def ship(src, dst_ref, send_sem, recv_sem, dev, is_self):
        @pl.when(is_self)
        def _():
            pltpu.make_async_copy(src, dst_ref, recv_sem).start()

        @pl.when(jnp.logical_not(is_self))
        def _():
            pltpu.make_async_remote_copy(
                src_ref=src, dst_ref=dst_ref, send_sem=send_sem, recv_sem=recv_sem,
                device_id=dev, device_id_type=MESH,
            ).start()

    def normalise(t, slot):
        for k in range(2):
            rows = pl.ds(k * TILE, TILE)
            u = xin[t, rows].astype(F32)
            xn[slot, rows] = (u * inv_rms(u)).astype(BF16)

    exchange_wait(1)
    normalise(1, 1)
    w_copies[0].wait()

    def b_project(i, carry):
        a = (x + ring_order(i)) % 4
        rows = xn[1]
        for t in range(3):
            m = nt(rows, wq[pl.ds(pl.multiple_of(t * D + a * 256, 256), 256), :])
            for cc in range(2):
                u = m[:, cc * HD : (cc + 1) * HD]
                h = 2 * a + cc
                if t < 2:
                    mixed[t, h] = u
                    u = u * inv_rms(u)
                sb[h, t] = u.astype(BF16).reshape(2, TILE, HD)
        for cc in range(2):
            h = 2 * a + cc
            ship(
                sb.at[h, pl.ds(0, 3)], rb.at[pl.ds(0, 3), pl.ds(2 * b_me, 2)],
                b_ss.at[h], b_rs.at[b_me], b_dev(h), h == b_me,
            )
        return carry

    lax.fori_loop(0, 4, b_project, 0)

    exchange_wait(0)
    normalise(0, 0)

    def f_project(i, carry):
        a = (y + ring_order(i)) % 4
        rows = xn[0]
        for t in range(3):
            m = nt(rows, wq[pl.ds(pl.multiple_of(t * D + a * 256, 256), 256), :])
            for cc in range(2):
                u = m[:, cc * HD : (cc + 1) * HD]
                if t < 2:
                    u = u * inv_rms(u)
                sf[2 * a + cc, t] = u.astype(BF16).reshape(2, TILE, HD)
        for cc in range(2):
            h = 2 * a + cc
            ship(
                sf.at[h], rf.at[:, pl.ds(2 * f_me, 2)],
                f_ss.at[h], f_rs.at[f_me], f_dev(h), h == f_me,
            )
        return carry

    lax.fori_loop(0, 4, f_project, 0)

    exchange_wait(2)
    w_copies[1].wait()

    def d_project(i, carry):
        a = (x + ring_order(i)) % 4
        m = nt(xin[2], wo[pl.ds(pl.multiple_of(a * 256, 256), 256), :])
        for cc in range(2):
            h = 2 * a + cc
            sb[h, 3] = m[:, cc * HD : (cc + 1) * HD].astype(BF16).reshape(2, TILE, HD)
            ship(
                sb.at[h, 3], rb.at[3, pl.ds(2 * b_me, 2)],
                d_ss.at[h], d_rs.at[b_me], b_dev(h), h == b_me,
            )
        return carry

    lax.fori_loop(0, 4, d_project, 0)

    def member_row(base, q):
        row = base + q * LIST
        return [lists[row + k] for k in range(5)]

    def weights_of(queries, keys, count):
        e = jnp.exp(nt(keys, queries) * FACTOR)
        parts = [e[:TILE]]
        for k in range(1, CAP):
            parts.append(e[k * TILE : (k + 1) * TILE] * jnp.where(count > k, 1.0, 0.0))
        e = jnp.concatenate(parts, axis=0)
        return e * (1.0 / jnp.sum(e, axis=0, keepdims=True))

    def stacked(ref, t, members):
        return jnp.concatenate([ref[t, members[k]] for k in range(CAP)], axis=0)

    for p in range(8):
        landed(rb.at[pl.ds(0, 3), pl.ds(2 * p, 2)], b_rs.at[p])
        landed(rb.at[3, pl.ds(2 * p, 2)], d_rs.at[p])

    def b_first(i, carry):
        p = ((x + ring_order(i // 2)) % 4) * 2 + i % 2
        for k in range(2):
            q = 2 * p + k
            m0, m1, m2, rank, count = member_row(GROUP * LIST, q)
            members = (m0, m1, m2)
            queries, grads = rb[0, q], rb[3, q]
            keys = stacked(rb, 1, members)
            values = stacked(rb, 2, members)
            soft = weights_of(queries, keys, count)
            low = soft.astype(BF16)
            grad_soft = nt(values, grads)
            delta = jnp.sum(low.astype(F32) * grad_soft, axis=0, keepdims=True)
            grad_scores = (soft * (grad_soft - delta)).astype(BF16)
            ptm[q] = low.reshape(CAP, TILE, HD)
            dst[q] = grad_scores.reshape(CAP, TILE, HD)
            bo[0, p, k] = (tn(grad_scores, keys) * FACTOR).astype(BF16)
        ship(bo.at[0, p], br.at[0, b_me], dq_ss.at[p], dq_rs.at[b_me], b_dev(p), p == b_me)
        return carry

    lax.fori_loop(0, 8, b_first, 0)

    def b_second(i, carry):
        p = ((x + ring_order(i // 2)) % 4) * 2 + i % 2
        for k in range(2):
            q = 2 * p + k
            m0, m1, m2, rank, count = member_row(GROUP * LIST, q)
            members = (m0, m1, m2)
            ds = jnp.concatenate([dst[m, rank] for m in members], axis=1)
            pt = jnp.concatenate([ptm[m, rank] for m in members], axis=1)
            bo[1, p, k] = (nn(ds, stacked(rb, 0, members)) * FACTOR).astype(BF16)
            bo[2, p, k] = nn(pt, stacked(rb, 3, members)).astype(BF16)
        ship(
            bo.at[pl.ds(1, 2), p], br.at[pl.ds(1, 2), b_me],
            dkv_ss.at[p], dkv_rs.at[b_me], b_dev(p), p == b_me,
        )
        return carry

    lax.fori_loop(0, 8, b_second, 0)

    for p in range(8):
        landed(rf.at[:, pl.ds(2 * p, 2)], f_rs.at[p])

    def f_attend(i, carry):
        p = ((y + ring_order(i // 2)) % 4) * 2 + i % 2
        for k in range(2):
            q = 2 * p + k
            m0, m1, m2, rank, count = member_row(0, q)
            members = (m0, m1, m2)
            low = weights_of(rf[0, q], stacked(rf, 1, members), count).astype(BF16)
            fo[p, k] = tn(low, stacked(rf, 2, members)).astype(BF16)
        ship(fo.at[p], fr.at[f_me], fo_ss.at[p], fo_rs.at[f_me], f_dev(p), p == f_me)
        return carry

    lax.fori_loop(0, 8, f_attend, 0)

    for h in range(HEADS):
        landed(fr.at[h], fo_rs.at[h])
        att[:, h * HD : (h + 1) * HD] = fr[h].reshape(2 * TILE, HD)

    def pipe_copy(result, k, out, dev, slot, send_sem, recv_sem):
        return pltpu.make_async_remote_copy(
            src_ref=res.at[result, pl.ds(k * TILE, TILE)],
            dst_ref=out.at[0, pl.ds(slot * TILE, TILE)],
            send_sem=send_sem.at[k], recv_sem=recv_sem.at[slot],
            device_id=dev, device_id_type=MESH,
        )

    def f_out(n, carry):
        cols = pl.ds(pl.multiple_of(n * 256, 256), 256)
        total = xin[0, :, cols].astype(F32) + nn(att[...], wo[:, cols])
        res[0, :, cols] = total.astype(BF16)
        return carry

    lax.fori_loop(0, 4, f_out, 0)

    @pl.when(z != 7)
    def _():
        for k in range(2):
            pipe_copy(0, k, on_hbm, (up, seq_of(2 * c + k, y, x // 2)), x % 2, pf_ss, pf_rs).start()

    def b_jacobian(i, carry):
        h = ((x + ring_order(i // 2)) % 4) * 2 + i % 2
        landed(br.at[0, h], dq_rs.at[h])
        landed(br.at[pl.ds(1, 2), h], dkv_rs.at[h])
        for t in range(2):
            u = mixed[t, h]
            r = inv_rms(u)
            unit = u * r
            g = br[t, h].reshape(2 * TILE, HD).astype(F32)
            back = r * (g - unit * jnp.mean(unit * g, axis=-1, keepdims=True))
            gm[:, pl.ds(pl.multiple_of(t * D + h * HD, HD), HD)] = back.astype(BF16)
        gm[:, pl.ds(pl.multiple_of(2 * D + h * HD, HD), HD)] = br[2, h].reshape(2 * TILE, HD)
        return carry

    lax.fori_loop(0, 8, b_jacobian, 0)

    def b_normed(n, carry):
        cols = pl.ds(pl.multiple_of(n * 256, 256), 256)
        gn[:, cols] = nn(gm[...], wq[:, cols])
        return carry

    lax.fori_loop(0, 4, b_normed, 0)

    for k in range(2):
        rows = pl.ds(k * TILE, TILE)
        u = xin[1, rows].astype(F32)
        r = inv_rms(u)
        unit = u * r
        g = gn[rows]
        back = r * (g - unit * jnp.mean(unit * g, axis=-1, keepdims=True))
        res[1, rows] = (xin[2, rows].astype(F32) + back).astype(BF16)

        @pl.when(z != 0)
        def _():
            pipe_copy(1, k, og_hbm, (down, seq_of(x, 2 * c + k, y // 2)), y % 2, pb_ss, pb_rs).start()

    for j in range(2):
        exchange_sent(0, j, True)
        exchange_sent(1, j, False)
        exchange_sent(2, j, False)

    def drain(h, carry):
        @pl.when(h != b_me)
        def _():
            landed(sb.at[h, pl.ds(0, 3)], b_ss.at[h])
            landed(sb.at[h, 3], d_ss.at[h])
            landed(bo.at[0, h], dq_ss.at[h])
            landed(bo.at[pl.ds(1, 2), h], dkv_ss.at[h])

        @pl.when(h != f_me)
        def _():
            landed(sf.at[h], f_ss.at[h])
            landed(fo.at[h], fo_ss.at[h])

        return carry

    lax.fori_loop(0, 8, drain, 0)

    @pl.when(z != 7)
    def _():
        for k in range(2):
            landed(res.at[0, pl.ds(k * TILE, TILE)], pf_ss.at[k])

    @pl.when(z != 0)
    def _():
        for k in range(2):
            landed(res.at[1, pl.ds(k * TILE, TILE)], pb_ss.at[k])
            landed(on_hbm.at[0, pl.ds(k * TILE, TILE)], pf_rs.at[k])

    @pl.when(z != 7)
    def _():
        for k in range(2):
            landed(og_hbm.at[0, pl.ds(k * TILE, TILE)], pb_rs.at[k])


def per_device(section_input, saved_input, grad_output, w_qkv, w_out, tile_cluster):
    any_spec = pl.BlockSpec(memory_space=pl.ANY)
    dma = pltpu.SemaphoreType.DMA
    block = jax.ShapeDtypeStruct((1, 2 * TILE, D), BF16)
    ahead, back = pl.pallas_call(
        kernel,
        out_shape=(block, block),
        in_specs=[pl.BlockSpec(memory_space=pltpu.SMEM)] + [any_spec] * 5,
        out_specs=(any_spec, any_spec),
        scratch_shapes=[
            pltpu.VMEM((3 * D, D), BF16),
            pltpu.VMEM((D, D), BF16),
            pltpu.VMEM((3, 2 * TILE, D), BF16),
            pltpu.VMEM((2, 2 * TILE, D), BF16),
            pltpu.VMEM((2, HEADS, 2 * TILE, HD), F32),
            pltpu.VMEM((HEADS, 3, 2, TILE, HD), BF16),
            pltpu.VMEM((HEADS, 4, 2, TILE, HD), BF16),
            pltpu.VMEM((3, GROUP + 1, TILE, HD), BF16),
            pltpu.VMEM((4, GROUP + 1, TILE, HD), BF16),
            pltpu.VMEM((GROUP + 1, CAP, TILE, HD), BF16),
            pltpu.VMEM((GROUP + 1, CAP, TILE, HD), BF16),
            pltpu.VMEM((HEADS, 2, TILE, HD), BF16),
            pltpu.VMEM((HEADS, 2, TILE, HD), BF16),
            pltpu.VMEM((3, HEADS, 2, TILE, HD), BF16),
            pltpu.VMEM((3, HEADS, 2, TILE, HD), BF16),
            pltpu.VMEM((2 * TILE, D), BF16),
            pltpu.VMEM((2 * TILE, 3 * D), BF16),
            pltpu.VMEM((2 * TILE, D), F32),
            pltpu.VMEM((2, 2 * TILE, D), BF16),
            pltpu.SMEM((2 * GROUP * LIST,), jnp.int32),
            dma((2,)), dma((3, 2)), dma((3, 2)),
            dma((8,)), dma((8,)), dma((8,)), dma((8,)), dma((8,)), dma((8,)),
            dma((8,)), dma((8,)), dma((8,)), dma((8,)), dma((8,)), dma((8,)),
            dma((2,)), dma((2,)), dma((2,)), dma((2,)),
        ],
        compiler_params=pltpu.CompilerParams(
            collective_id=0, has_side_effects=True, vmem_limit_bytes=56 * 2**20
        ),
    )(tile_cluster, section_input, saved_input, grad_output, w_qkv, w_out)
    z = lax.axis_index("pipe")
    nothing = jnp.zeros((), BF16)
    return (
        jnp.where(z == 0, nothing, ahead),
        jnp.where(z == lax.axis_size("pipe") - 1, nothing, back),
    )


def solution(mesh):
    return jax.shard_map(
        per_device,
        mesh=mesh,
        in_specs=(
            P("pipe", "seq", None),
            P("pipe", "seq", None),
            P("pipe", "seq", None),
            P("pipe", None, None),
            P("pipe", None, None),
            P(),
        ),
        out_specs=(P("pipe", "seq", None), P("pipe", "seq", None)),
        check_vma=False,
    )
```

```python
import jax
import jax.numpy as jnp
from jax import lax
from jax.experimental import pallas as pl
from jax.experimental.pallas import tpu as pltpu
from jax.sharding import PartitionSpec as P

MESH = pl.DeviceIdType.MESH
HEADS = 8
HD = 128
TILE = 128
D = 1024
GROUP = 16
CAP = 3
LIST = 8
EPS = 1e-05
FACTOR = HD ** (-0.5)
F32 = jnp.float32
BF16 = jnp.bfloat16


def nt(a, b):
    return lax.dot_general(a, b, (((1,), (1,)), ((), ())), preferred_element_type=F32)


def tn(a, b):
    return lax.dot_general(a, b, (((0,), (0,)), ((), ())), preferred_element_type=F32)


def nn(a, b):
    return jnp.dot(a, b, preferred_element_type=F32)


def inv_rms(u):
    return lax.rsqrt(jnp.mean(u * u, axis=-1, keepdims=True) + EPS)


def ring_order(i):
    return (1 + 2 * i - 3 * (i // 2)) % 4


def landed(ref, sem):
    pltpu.make_async_copy(ref, ref, sem).wait()


def kernel(
    tc_ref, x_hbm, xs_hbm, g_hbm, wq_hbm, wo_hbm,
    on_hbm, og_hbm,
    wq, wo, xin, xn, mixed, sf, sb, rf, rb, rd, soft, dst, ptm, fo, fr, bo, br, att, gm, gn, res,
    lists,
    w_sem, ex_ss, ex_rs, f_ss, f_rs, b_ss, b_rs, d_ss, d_rs,
    fo_ss, fo_rs, dq_ss, dq_rs, dkv_ss, dkv_rs, pf_ss, pf_rs, pb_ss, pb_rs,
):
    z = lax.axis_index("pipe")
    s = lax.axis_index("seq")
    y = s // 8
    x = (s // 2) % 4
    c = s % 2

    def seq_of(xx, yy, cc):
        return (yy * 4 + xx) * 2 + cc

    def f_dev(h):
        return (z, seq_of(x, h // 2, h % 2))

    def b_dev(h):
        return (z, seq_of(h // 2, y, h % 2))

    f_me = y * 2 + c
    b_me = x * 2 + c
    up = (z + 1) % 8
    down = (z + 7) % 8

    w_copies = [
        pltpu.make_async_copy(wq_hbm.at[0], wq, w_sem.at[0]),
        pltpu.make_async_copy(wo_hbm.at[0], wo, w_sem.at[1]),
    ]
    for copy in w_copies:
        copy.start()

    barrier = pltpu.get_barrier_semaphore()

    def greet(dev):
        pl.semaphore_signal(barrier, inc=1, device_id=dev, device_id_type=MESH)

    for i in range(1, 8):
        greet(f_dev((f_me + i) % 8))
    for i in range(2, 8):
        greet(b_dev((2 * x + i) % 8))
    for k in range(2):
        for zz in (up, down):
            greet((zz, seq_of(2 * c + k, y, x // 2)))
            greet((zz, seq_of(x, 2 * c + k, y // 2)))
    pl.semaphore_wait(barrier, 21)

    def exchange(t, src_hbm, j, forward):
        other = 2 * c + j
        own = x if forward else y
        dev = (z, seq_of(other, y, x // 2) if forward else seq_of(x, other, y // 2))
        src = src_hbm.at[0, pl.ds(j * TILE, TILE)]
        slot = (own + j) % 2
        dst_ref = xin.at[t, pl.ds(slot * TILE, TILE)]
        recv = ex_rs.at[t, slot]

        @pl.when(own == other)
        def _():
            pltpu.make_async_copy(src, dst_ref, recv).start()

        @pl.when(own != other)
        def _():
            pltpu.make_async_remote_copy(
                src_ref=src, dst_ref=dst_ref, send_sem=ex_ss.at[t, j], recv_sem=recv,
                device_id=dev, device_id_type=MESH,
            ).start()

    def exchange_sent(t, j, forward):
        own = x if forward else y

        @pl.when(own != 2 * c + j)
        def _():
            landed(xin.at[t, pl.ds(j * TILE, TILE)], ex_ss.at[t, j])

    def exchange_wait(t):
        for k in range(2):
            landed(xin.at[t, pl.ds(k * TILE, TILE)], ex_rs.at[t, k])

    for j in range(2):
        exchange(1, xs_hbm, j, False)
        exchange(0, x_hbm, j, True)
    def f_source(k):
        return 2 * c + (k + x) % 2

    def b_source(k):
        return 2 * c + (k + y) % 2

    def fill(base, tile_of):
        ids = [tc_ref[tile_of(q)] for q in range(GROUP)]

        def one(q, carry):
            own_id = tc_ref[tile_of(q)]
            count = jnp.int32(0)
            rank = jnp.int32(0)
            members = [jnp.int32(GROUP)] * CAP
            for p in range(GROUP):
                same = ids[p] == own_id
                members = [
                    jnp.where(same & (count == k), p, members[k]) for k in range(CAP)
                ]
                rank = rank + jnp.where(same & (p < q), 1, 0)
                count = count + jnp.where(same, 1, 0)
            row = base + q * LIST
            for k in range(CAP):
                lists[row + k] = members[k]
            lists[row + 3] = jnp.minimum(rank, CAP - 1)
            lists[row + 4] = count
            return carry

        lax.fori_loop(0, GROUP, one, 0)

    fill(0, lambda q: 4 * ((q // 2) * 2 + (q + x) % 2) + x)
    fill(GROUP * LIST, lambda q: 4 * ((((q // 2) % 2) * 2 + (q + y) % 2) * 4 + q // 4) + y)

    zero = jnp.zeros((TILE, HD), BF16)
    for t in range(3):
        rf[t, GROUP] = zero
        rb[t, GROUP] = zero
    rd[GROUP] = zero
    for k in range(CAP):
        dst[GROUP, k] = zero
        ptm[GROUP, k] = zero

    def ship(src, dst_ref, send_sem, recv_sem, dev, is_self):
        @pl.when(is_self)
        def _():
            pltpu.make_async_copy(src, dst_ref, recv_sem).start()

        @pl.when(jnp.logical_not(is_self))
        def _():
            pltpu.make_async_remote_copy(
                src_ref=src, dst_ref=dst_ref, send_sem=send_sem, recv_sem=recv_sem,
                device_id=dev, device_id_type=MESH,
            ).start()

    def normalise(t, slot):
        for k in range(2):
            rows = pl.ds(k * TILE, TILE)
            u = xin[t, rows].astype(F32)
            xn[slot, rows] = (u * inv_rms(u)).astype(BF16)

    exchange_wait(1)
    for j in range(2):
        exchange(2, g_hbm, j, False)
    normalise(1, 1)
    w_copies[0].wait()

    def b_project(i, carry):
        a = (x + ring_order(i)) % 4
        rows = xn[1]
        for t in range(3):
            m = nt(rows, wq[pl.ds(pl.multiple_of(t * D + a * 256, 256), 256), :])
            for cc in range(2):
                u = m[:, cc * HD : (cc + 1) * HD]
                h = 2 * a + cc
                if t < 2:
                    mixed[t, h] = u
                    u = u * inv_rms(u)
                sb[h, t] = u.astype(BF16).reshape(2, TILE, HD)
        for cc in range(2):
            h = 2 * a + cc
            ship(
                sb.at[h, pl.ds(0, 3)], rb.at[:, pl.ds(2 * b_me, 2)],
                b_ss.at[h], b_rs.at[b_me], b_dev(h), h == b_me,
            )
        return carry

    lax.fori_loop(0, 4, b_project, 0)

    exchange_wait(0)
    normalise(0, 0)

    def f_project(i, carry):
        a = (y + ring_order(i)) % 4
        rows = xn[0]
        for t in range(3):
            m = nt(rows, wq[pl.ds(pl.multiple_of(t * D + a * 256, 256), 256), :])
            for cc in range(2):
                u = m[:, cc * HD : (cc + 1) * HD]
                if t < 2:
                    u = u * inv_rms(u)
                sf[2 * a + cc, t] = u.astype(BF16).reshape(2, TILE, HD)
        for cc in range(2):
            h = 2 * a + cc
            ship(
                sf.at[h], rf.at[:, pl.ds(2 * f_me, 2)],
                f_ss.at[h], f_rs.at[f_me], f_dev(h), h == f_me,
            )
        return carry

    lax.fori_loop(0, 4, f_project, 0)

    exchange_wait(2)
    w_copies[1].wait()

    def d_project(i, carry):
        a = (x + ring_order(i)) % 4
        m = nt(xin[2], wo[pl.ds(pl.multiple_of(a * 256, 256), 256), :])
        for cc in range(2):
            h = 2 * a + cc
            sb[h, 3] = m[:, cc * HD : (cc + 1) * HD].astype(BF16).reshape(2, TILE, HD)
            ship(
                sb.at[h, 3], rd.at[pl.ds(2 * b_me, 2)],
                d_ss.at[h], d_rs.at[b_me], b_dev(h), h == b_me,
            )
        return carry

    lax.fori_loop(0, 4, d_project, 0)

    def member_row(base, q):
        row = base + q * LIST
        return [lists[row + k] for k in range(5)]

    def weights_of(queries, keys, count):
        e = jnp.exp(nt(queries, keys) * FACTOR)
        parts = [e[:, :TILE]]
        for k in range(1, CAP):
            parts.append(e[:, k * TILE : (k + 1) * TILE] * jnp.where(count > k, 1.0, 0.0))
        total = jnp.sum(parts[0] + parts[1] + parts[2], axis=1, keepdims=True)
        return jnp.concatenate(parts, axis=1) * (1.0 / total)

    def stacked(ref, t, members):
        return jnp.concatenate([ref[t, m] for m in members], axis=0)

    for p in range(8):
        landed(rb.at[:, pl.ds(2 * p, 2)], b_rs.at[p])

    def b_soft(i, carry):
        for k in range(4):
            q = 4 * i + k
            m0, m1, m2, rank, count = member_row(GROUP * LIST, q)
            soft[q] = weights_of(rb[0, q], stacked(rb, 1, (m0, m1, m2)), count)
        return carry

    lax.fori_loop(0, 4, b_soft, 0)

    for p in range(8):
        landed(rd.at[pl.ds(2 * p, 2)], d_rs.at[p])

    def b_first(i, carry):
        a = (x + ring_order(i)) % 4
        for k in range(4):
            p = 2 * a + k // 2
            q = 4 * a + k
            m0, m1, m2, rank, count = member_row(GROUP * LIST, q)
            members = (m0, m1, m2)
            grad_soft = nt(rd[q], stacked(rb, 2, members))
            weights = soft[q]
            low = weights.astype(BF16)
            delta = jnp.sum(low.astype(F32) * grad_soft, axis=1, keepdims=True)
            grad_scores = (weights * (grad_soft - delta)).astype(BF16)
            for n in range(CAP):
                ptm[q, n] = low[:, n * TILE : (n + 1) * TILE]
                dst[q, n] = grad_scores[:, n * TILE : (n + 1) * TILE]
            bo[0, p, k % 2] = (nn(grad_scores, stacked(rb, 1, members)) * FACTOR).astype(BF16)
        for cc in range(2):
            p = 2 * a + cc
            ship(bo.at[0, p], br.at[0, b_me], dq_ss.at[p], dq_rs.at[b_me], b_dev(p), p == b_me)
        return carry

    lax.fori_loop(0, 4, b_first, 0)

    for p in range(8):
        landed(rf.at[:, pl.ds(2 * p, 2)], f_rs.at[p])

    def f_attend(i, carry):
        a = (y + ring_order(i)) % 4
        for k in range(4):
            q = 4 * a + k
            m0, m1, m2, rank, count = member_row(0, q)
            members = (m0, m1, m2)
            low = weights_of(rf[0, q], stacked(rf, 1, members), count).astype(BF16)
            fo[2 * a + k // 2, k % 2] = nn(low, stacked(rf, 2, members)).astype(BF16)
        for cc in range(2):
            p = 2 * a + cc
            ship(fo.at[p], fr.at[f_me], fo_ss.at[p], fo_rs.at[f_me], f_dev(p), p == f_me)
        return carry

    lax.fori_loop(0, 4, f_attend, 0)

    def b_second(i, carry):
        k = i // 4
        a = (x + ring_order(i % 4)) % 4
        for cc in range(2):
            p = 2 * a + cc
            q = 2 * p + k
            m0, m1, m2, rank, count = member_row(GROUP * LIST, q)
            members = (m0, m1, m2)
            ds = jnp.concatenate([dst[m, rank] for m in members], axis=0)
            pt = jnp.concatenate([ptm[m, rank] for m in members], axis=0)
            bo[1, p, k] = (tn(ds, stacked(rb, 0, members)) * FACTOR).astype(BF16)
            bo[2, p, k] = tn(pt, jnp.concatenate([rd[m] for m in members], axis=0)).astype(BF16)
        for cc in range(2):
            p = 2 * a + cc
            ship(
                bo.at[pl.ds(1, 2), p, k], br.at[pl.ds(1, 2), b_me, k],
                dkv_ss.at[k, p], dkv_rs.at[k, b_me], b_dev(p), p == b_me,
            )
        return carry

    lax.fori_loop(0, 8, b_second, 0)

    for h in range(HEADS):
        landed(fr.at[h], fo_rs.at[h])
        att[:, h * HD : (h + 1) * HD] = fr[h].reshape(2 * TILE, HD)

    def f_result(k):
        rows = pl.ds(k * TILE, TILE)

        def columns(n, carry):
            cols = pl.ds(pl.multiple_of(n * 256, 256), 256)
            total = xin[0, rows, cols].astype(F32) + nn(att[rows], wo[:, cols])
            res[0, rows, cols] = total.astype(BF16)
            return carry

        lax.fori_loop(0, 4, columns, 0)

    def pipe_start(result, k, out, dev, slot, send_sem, recv_sem):
        pltpu.make_async_remote_copy(
            src_ref=res.at[result, pl.ds(k * TILE, TILE)],
            dst_ref=out.at[0, pl.ds(slot * TILE, TILE)],
            send_sem=send_sem.at[k], recv_sem=recv_sem.at[slot],
            device_id=dev, device_id_type=MESH,
        ).start()

    def f_leave(k):
        @pl.when(z != 7)
        def _():
            pipe_start(0, k, on_hbm, (up, seq_of(f_source(k), y, x // 2)), x % 2, pf_ss, pf_rs)

    f_result(0)
    f_leave(0)
    f_result(1)

    def jacobian(t, h, k):
        u = mixed[t, h, pl.ds(k * TILE, TILE)]
        r = inv_rms(u)
        unit = u * r
        g = br[t, h, k].astype(F32)
        back = r * (g - unit * jnp.mean(unit * g, axis=-1, keepdims=True))
        gm[k, :, pl.ds(pl.multiple_of(t * D + h * HD, HD), HD)] = back.astype(BF16)

    def b_queries(i, carry):
        h = ((x + ring_order(i // 2)) % 4) * 2 + i % 2
        landed(br.at[0, h], dq_rs.at[h])
        for k in range(2):
            jacobian(0, h, k)
        return carry

    lax.fori_loop(0, 8, b_queries, 0)

    def b_query_part(n, carry):
        cols = pl.ds(pl.multiple_of(n * 256, 256), 256)
        for k in range(2):
            gn[k, :, cols] = nn(gm[k, :, :D], wq[:D, cols])
        return carry

    lax.fori_loop(0, 4, b_query_part, 0)

    for k in range(2):
        for h in range(8):
            landed(br.at[pl.ds(1, 2), h, k], dkv_rs.at[k, h])
        if k == 1:
            f_leave(1)

        def b_keys(h, carry):
            jacobian(1, h, k)
            gm[k, :, pl.ds(pl.multiple_of(2 * D + h * HD, HD), HD)] = br[2, h, k]
            return carry

        lax.fori_loop(0, 8, b_keys, 0)

        def b_normed(n, carry):
            cols = pl.ds(pl.multiple_of(n * 256, 256), 256)
            gn[k, :, cols] += nn(gm[k, :, D:], wq[D:, cols])
            return carry

        lax.fori_loop(0, 4, b_normed, 0)
        rows = pl.ds(k * TILE, TILE)
        u = xin[1, rows].astype(F32)
        r = inv_rms(u)
        unit = u * r
        g = gn[k]
        back = r * (g - unit * jnp.mean(unit * g, axis=-1, keepdims=True))
        res[1, rows] = (xin[2, rows].astype(F32) + back).astype(BF16)

        @pl.when(z != 0)
        def _():
            pipe_start(1, k, og_hbm, (down, seq_of(x, b_source(k), y // 2)), y % 2, pb_ss, pb_rs)

    for j in range(2):
        exchange_sent(0, j, True)
        exchange_sent(1, j, False)
        exchange_sent(2, j, False)

    def drain(h, carry):
        @pl.when(h != b_me)
        def _():
            landed(sb.at[h, pl.ds(0, 3)], b_ss.at[h])
            landed(sb.at[h, 3], d_ss.at[h])
            landed(bo.at[0, h], dq_ss.at[h])
            for k in range(2):
                landed(bo.at[pl.ds(1, 2), h, k], dkv_ss.at[k, h])

        @pl.when(h != f_me)
        def _():
            landed(sf.at[h], f_ss.at[h])
            landed(fo.at[h], fo_ss.at[h])

        return carry

    lax.fori_loop(0, 8, drain, 0)

    @pl.when(z != 7)
    def _():
        for k in range(2):
            landed(res.at[0, pl.ds(k * TILE, TILE)], pf_ss.at[k])

    @pl.when(z != 0)
    def _():
        for k in range(2):
            landed(res.at[1, pl.ds(k * TILE, TILE)], pb_ss.at[k])
            landed(on_hbm.at[0, pl.ds(k * TILE, TILE)], pf_rs.at[k])

    @pl.when(z != 7)
    def _():
        for k in range(2):
            landed(og_hbm.at[0, pl.ds(k * TILE, TILE)], pb_rs.at[k])


def per_device(section_input, saved_input, grad_output, w_qkv, w_out, tile_cluster):
    any_spec = pl.BlockSpec(memory_space=pl.ANY)
    dma = pltpu.SemaphoreType.DMA
    block = jax.ShapeDtypeStruct((1, 2 * TILE, D), BF16)
    ahead, back = pl.pallas_call(
        kernel,
        out_shape=(block, block),
        in_specs=[pl.BlockSpec(memory_space=pltpu.SMEM)] + [any_spec] * 5,
        out_specs=(any_spec, any_spec),
        scratch_shapes=[
            pltpu.VMEM((3 * D, D), BF16),
            pltpu.VMEM((D, D), BF16),
            pltpu.VMEM((3, 2 * TILE, D), BF16),
            pltpu.VMEM((2, 2 * TILE, D), BF16),
            pltpu.VMEM((2, HEADS, 2 * TILE, HD), F32),
            pltpu.VMEM((HEADS, 3, 2, TILE, HD), BF16),
            pltpu.VMEM((HEADS, 4, 2, TILE, HD), BF16),
            pltpu.VMEM((3, GROUP + 1, TILE, HD), BF16),
            pltpu.VMEM((3, GROUP + 1, TILE, HD), BF16),
            pltpu.VMEM((GROUP + 1, TILE, HD), BF16),
            pltpu.VMEM((GROUP, TILE, CAP * TILE), F32),
            pltpu.VMEM((GROUP + 1, CAP, TILE, HD), BF16),
            pltpu.VMEM((GROUP + 1, CAP, TILE, HD), BF16),
            pltpu.VMEM((HEADS, 2, TILE, HD), BF16),
            pltpu.VMEM((HEADS, 2, TILE, HD), BF16),
            pltpu.VMEM((3, HEADS, 2, TILE, HD), BF16),
            pltpu.VMEM((3, HEADS, 2, TILE, HD), BF16),
            pltpu.VMEM((2 * TILE, D), BF16),
            pltpu.VMEM((2, TILE, 3 * D), BF16),
            pltpu.VMEM((2, TILE, D), F32),
            pltpu.VMEM((2, 2 * TILE, D), BF16),
            pltpu.SMEM((2 * GROUP * LIST,), jnp.int32),
            dma((2,)), dma((3, 2)), dma((3, 2)),
            dma((8,)), dma((8,)), dma((8,)), dma((8,)), dma((8,)), dma((8,)),
            dma((8,)), dma((8,)), dma((8,)), dma((8,)), dma((2, 8)), dma((2, 8)),
            dma((2,)), dma((2,)), dma((2,)), dma((2,)),
        ],
        compiler_params=pltpu.CompilerParams(
            collective_id=0, has_side_effects=True, vmem_limit_bytes=56 * 2**20
        ),
    )(tile_cluster, section_input, saved_input, grad_output, w_qkv, w_out)
    z = lax.axis_index("pipe")
    nothing = jnp.zeros((), BF16)
    return (
        jnp.where(z == 0, nothing, ahead),
        jnp.where(z == lax.axis_size("pipe") - 1, nothing, back),
    )


def solution(mesh):
    return jax.shard_map(
        per_device,
        mesh=mesh,
        in_specs=(
            P("pipe", "seq", None),
            P("pipe", "seq", None),
            P("pipe", "seq", None),
            P("pipe", None, None),
            P("pipe", None, None),
            P(),
        ),
        out_specs=(P("pipe", "seq", None), P("pipe", "seq", None)),
        check_vma=False,
    )
```

```python
import jax
import jax.numpy as jnp
from jax import lax
from jax.experimental import pallas as pl
from jax.experimental.pallas import tpu as pltpu
from jax.sharding import PartitionSpec as P

MESH = pl.DeviceIdType.MESH
HEADS = 8
HD = 128
TILE = 128
D = 1024
GROUP = 16
CAP = 3
LIST = 8
EPS = 1e-05
FACTOR = HD ** (-0.5)
F32 = jnp.float32
BF16 = jnp.bfloat16


def nt(a, b):
    return lax.dot_general(a, b, (((1,), (1,)), ((), ())), preferred_element_type=F32)


def tn(a, b):
    return lax.dot_general(a, b, (((0,), (0,)), ((), ())), preferred_element_type=F32)


def nn(a, b):
    return jnp.dot(a, b, preferred_element_type=F32)


def inv_rms(u):
    return lax.rsqrt(jnp.mean(u * u, axis=-1, keepdims=True) + EPS)


def ring_order(i):
    return (1 + 2 * i - 3 * (i // 2)) % 4


def landed(ref, sem):
    pltpu.make_async_copy(ref, ref, sem).wait()


def kernel(
    tc_ref, x_hbm, xs_hbm, g_hbm, wq_hbm, wo_hbm,
    on_hbm, og_hbm,
    wq, wo, xin, xn, mixed, sf, sb, rf, rb, rd, soft, dst, ptm, fo, fr, bo, br, att, gm, gn, res,
    lists,
    w_sem, ex_ss, ex_rs, f_ss, f_rs, b_ss, b_rs, d_ss, d_rs,
    fo_ss, fo_rs, dq_ss, dq_rs, dkv_ss, dkv_rs, pf_ss, pf_rs, pb_ss, pb_rs,
):
    z = lax.axis_index("pipe")
    s = lax.axis_index("seq")
    y = s // 8
    x = (s // 2) % 4
    c = s % 2

    def seq_of(xx, yy, cc):
        return (yy * 4 + xx) * 2 + cc

    def f_dev(h):
        return (z, seq_of(x, h // 2, h % 2))

    def b_dev(h):
        return (z, seq_of(h // 2, y, h % 2))

    f_me = y * 2 + c
    b_me = x * 2 + c
    up = (z + 1) % 8
    down = (z + 7) % 8

    w_copies = [
        pltpu.make_async_copy(wq_hbm.at[0], wq, w_sem.at[0]),
        pltpu.make_async_copy(wo_hbm.at[0], wo, w_sem.at[1]),
    ]
    for copy in w_copies:
        copy.start()

    barrier = pltpu.get_barrier_semaphore()

    def greet(dev):
        pl.semaphore_signal(barrier, inc=1, device_id=dev, device_id_type=MESH)

    for i in range(1, 8):
        greet(f_dev((f_me + i) % 8))
    for i in range(2, 8):
        greet(b_dev((2 * x + i) % 8))
    for k in range(2):
        for zz in (up, down):
            greet((zz, seq_of(2 * c + k, y, x // 2)))
            greet((zz, seq_of(x, 2 * c + k, y // 2)))
    pl.semaphore_wait(barrier, 21)

    def exchange(t, src_hbm, j, forward):
        other = 2 * c + j
        own = x if forward else y
        dev = (z, seq_of(other, y, x // 2) if forward else seq_of(x, other, y // 2))
        src = src_hbm.at[0, pl.ds(j * TILE, TILE)]
        slot = (own + j) % 2
        dst_ref = xin.at[t, pl.ds(slot * TILE, TILE)]
        recv = ex_rs.at[t, slot]

        @pl.when(own == other)
        def _():
            pltpu.make_async_copy(src, dst_ref, recv).start()

        @pl.when(own != other)
        def _():
            pltpu.make_async_remote_copy(
                src_ref=src, dst_ref=dst_ref, send_sem=ex_ss.at[t, j], recv_sem=recv,
                device_id=dev, device_id_type=MESH,
            ).start()

    def exchange_sent(t, j, forward):
        own = x if forward else y

        @pl.when(own != 2 * c + j)
        def _():
            landed(xin.at[t, pl.ds(j * TILE, TILE)], ex_ss.at[t, j])

    def exchange_wait(t):
        for k in range(2):
            landed(xin.at[t, pl.ds(k * TILE, TILE)], ex_rs.at[t, k])

    for j in range(2):
        exchange(1, xs_hbm, j, False)
        exchange(0, x_hbm, j, True)
    def f_source(k):
        return 2 * c + (k + x) % 2

    def b_source(k):
        return 2 * c + (k + y) % 2

    def fill(base, tile_of):
        ids = [tc_ref[tile_of(q)] for q in range(GROUP)]

        def one(q, carry):
            own_id = tc_ref[tile_of(q)]
            count = jnp.int32(0)
            rank = jnp.int32(0)
            members = [jnp.int32(GROUP)] * CAP
            for p in range(GROUP):
                same = ids[p] == own_id
                members = [
                    jnp.where(same & (count == k), p, members[k]) for k in range(CAP)
                ]
                rank = rank + jnp.where(same & (p < q), 1, 0)
                count = count + jnp.where(same, 1, 0)
            row = base + q * LIST
            for k in range(CAP):
                lists[row + k] = members[k]
            lists[row + 3] = jnp.minimum(rank, CAP - 1)
            lists[row + 4] = count
            return carry

        lax.fori_loop(0, GROUP, one, 0)

    fill(0, lambda q: 4 * ((q // 2) * 2 + (q + x) % 2) + x)
    fill(GROUP * LIST, lambda q: 4 * ((((q // 2) % 2) * 2 + (q + y) % 2) * 4 + q // 4) + y)

    zero = jnp.zeros((TILE, HD), BF16)
    for t in range(3):
        rf[t, GROUP] = zero
        rb[t, GROUP] = zero
    rd[GROUP] = zero
    for k in range(CAP):
        dst[GROUP, k] = zero
        ptm[GROUP, k] = zero

    def ship(src, dst_ref, send_sem, recv_sem, dev, is_self):
        @pl.when(is_self)
        def _():
            pltpu.make_async_copy(src, dst_ref, recv_sem).start()

        @pl.when(jnp.logical_not(is_self))
        def _():
            pltpu.make_async_remote_copy(
                src_ref=src, dst_ref=dst_ref, send_sem=send_sem, recv_sem=recv_sem,
                device_id=dev, device_id_type=MESH,
            ).start()

    def normalise(t, slot):
        for k in range(2):
            rows = pl.ds(k * TILE, TILE)
            u = xin[t, rows].astype(F32)
            xn[slot, rows] = (u * inv_rms(u)).astype(BF16)

    exchange_wait(1)
    for j in range(2):
        exchange(2, g_hbm, j, False)
    normalise(1, 1)
    w_copies[0].wait()

    def b_project(i, carry):
        a = (x + ring_order(i)) % 4
        rows = xn[1]
        for t in range(3):
            m = nt(rows, wq[pl.ds(pl.multiple_of(t * D + a * 256, 256), 256), :])
            for cc in range(2):
                u = m[:, cc * HD : (cc + 1) * HD]
                h = 2 * a + cc
                if t < 2:
                    mixed[t, h] = u
                    u = u * inv_rms(u)
                sb[h, t] = u.astype(BF16).reshape(2, TILE, HD)
        for cc in range(2):
            h = 2 * a + cc
            ship(
                sb.at[h, pl.ds(0, 3)], rb.at[:, pl.ds(2 * b_me, 2)],
                b_ss.at[h], b_rs.at[b_me], b_dev(h), h == b_me,
            )
        return carry

    lax.fori_loop(0, 4, b_project, 0)

    exchange_wait(0)
    normalise(0, 0)

    def f_project(i, carry):
        a = (y + ring_order(i)) % 4
        rows = xn[0]
        for t in range(3):
            m = nt(rows, wq[pl.ds(pl.multiple_of(t * D + a * 256, 256), 256), :])
            for cc in range(2):
                u = m[:, cc * HD : (cc + 1) * HD]
                if t < 2:
                    u = u * inv_rms(u)
                sf[2 * a + cc, t] = u.astype(BF16).reshape(2, TILE, HD)
        for cc in range(2):
            h = 2 * a + cc
            ship(
                sf.at[h], rf.at[:, pl.ds(2 * f_me, 2)],
                f_ss.at[h], f_rs.at[f_me], f_dev(h), h == f_me,
            )
        return carry

    lax.fori_loop(0, 4, f_project, 0)

    exchange_wait(2)
    w_copies[1].wait()

    def d_project(i, carry):
        a = (x + ring_order(i)) % 4
        m = nt(xin[2], wo[pl.ds(pl.multiple_of(a * 256, 256), 256), :])
        for cc in range(2):
            h = 2 * a + cc
            sb[h, 3] = m[:, cc * HD : (cc + 1) * HD].astype(BF16).reshape(2, TILE, HD)
            ship(
                sb.at[h, 3], rd.at[pl.ds(2 * b_me, 2)],
                d_ss.at[h], d_rs.at[b_me], b_dev(h), h == b_me,
            )
        return carry

    lax.fori_loop(0, 4, d_project, 0)

    def member_row(base, q):
        row = base + q * LIST
        return [lists[row + k] for k in range(5)]

    def weights_of(queries, keys, count):
        e = jnp.exp(nt(queries, keys) * FACTOR)
        parts = [e[:, :TILE]]
        for k in range(1, CAP):
            parts.append(e[:, k * TILE : (k + 1) * TILE] * jnp.where(count > k, 1.0, 0.0))
        total = jnp.sum(parts[0] + parts[1] + parts[2], axis=1, keepdims=True)
        return jnp.concatenate(parts, axis=1) * (1.0 / total)

    def stacked(ref, t, members):
        return jnp.concatenate([ref[t, m] for m in members], axis=0)

    for p in range(8):
        landed(rb.at[:, pl.ds(2 * p, 2)], b_rs.at[p])

    def b_soft(i, carry):
        for k in range(4):
            q = 4 * i + k
            m0, m1, m2, rank, count = member_row(GROUP * LIST, q)
            soft[q] = weights_of(rb[0, q], stacked(rb, 1, (m0, m1, m2)), count)
        return carry

    lax.fori_loop(0, 4, b_soft, 0)

    for p in range(8):
        landed(rd.at[pl.ds(2 * p, 2)], d_rs.at[p])

    def b_first(i, carry):
        a = (x + ring_order(i)) % 4
        for k in range(4):
            p = 2 * a + k // 2
            q = 4 * a + k
            m0, m1, m2, rank, count = member_row(GROUP * LIST, q)
            members = (m0, m1, m2)
            grad_soft = nt(rd[q], stacked(rb, 2, members))
            weights = soft[q]
            low = weights.astype(BF16)
            delta = jnp.sum(low.astype(F32) * grad_soft, axis=1, keepdims=True)
            grad_scores = (weights * (grad_soft - delta)).astype(BF16)
            for n in range(CAP):
                ptm[q, n] = low[:, n * TILE : (n + 1) * TILE]
                dst[q, n] = grad_scores[:, n * TILE : (n + 1) * TILE]
            bo[0, p, k % 2] = (nn(grad_scores, stacked(rb, 1, members)) * FACTOR).astype(BF16)
        for cc in range(2):
            p = 2 * a + cc
            ship(bo.at[0, p], br.at[0, b_me], dq_ss.at[p], dq_rs.at[b_me], b_dev(p), p == b_me)
        return carry

    lax.fori_loop(0, 4, b_first, 0)

    for p in range(8):
        landed(rf.at[:, pl.ds(2 * p, 2)], f_rs.at[p])

    def f_attend(i, carry):
        a = (y + ring_order(i)) % 4
        for k in range(4):
            q = 4 * a + k
            m0, m1, m2, rank, count = member_row(0, q)
            members = (m0, m1, m2)
            low = weights_of(rf[0, q], stacked(rf, 1, members), count).astype(BF16)
            fo[2 * a + k // 2, k % 2] = nn(low, stacked(rf, 2, members)).astype(BF16)
        for cc in range(2):
            p = 2 * a + cc
            ship(fo.at[p], fr.at[f_me], fo_ss.at[p], fo_rs.at[f_me], f_dev(p), p == f_me)
        return carry

    lax.fori_loop(0, 4, f_attend, 0)

    def b_second(i, carry):
        k = i // 4
        a = (x + ring_order(i % 4)) % 4
        for cc in range(2):
            p = 2 * a + cc
            q = 2 * p + k
            m0, m1, m2, rank, count = member_row(GROUP * LIST, q)
            members = (m0, m1, m2)
            ds = jnp.concatenate([dst[m, rank] for m in members], axis=0)
            pt = jnp.concatenate([ptm[m, rank] for m in members], axis=0)
            bo[1, p, k] = (tn(ds, stacked(rb, 0, members)) * FACTOR).astype(BF16)
            bo[2, p, k] = tn(pt, jnp.concatenate([rd[m] for m in members], axis=0)).astype(BF16)
        for cc in range(2):
            p = 2 * a + cc
            ship(
                bo.at[pl.ds(1, 2), p, k], br.at[pl.ds(1, 2), b_me, k],
                dkv_ss.at[k, p], dkv_rs.at[k, b_me], b_dev(p), p == b_me,
            )
        return carry

    lax.fori_loop(0, 8, b_second, 0)

    for h in range(HEADS):
        landed(fr.at[h], fo_rs.at[h])
        att[:, h * HD : (h + 1) * HD] = fr[h].reshape(2 * TILE, HD)

    def f_result(k):
        rows = pl.ds(k * TILE, TILE)

        def columns(n, carry):
            cols = pl.ds(pl.multiple_of(n * 256, 256), 256)
            total = xin[0, rows, cols].astype(F32) + nn(att[rows], wo[:, cols])
            res[0, rows, cols] = total.astype(BF16)
            return carry

        lax.fori_loop(0, 4, columns, 0)

    def pipe_start(result, k, out, dev, slot, send_sem, recv_sem):
        pltpu.make_async_remote_copy(
            src_ref=res.at[result, pl.ds(k * TILE, TILE)],
            dst_ref=out.at[0, pl.ds(slot * TILE, TILE)],
            send_sem=send_sem.at[k], recv_sem=recv_sem.at[slot],
            device_id=dev, device_id_type=MESH,
        ).start()

    def f_leave(k):
        @pl.when(z != 7)
        def _():
            pipe_start(0, k, on_hbm, (up, seq_of(f_source(k), y, x // 2)), x % 2, pf_ss, pf_rs)

    f_result(0)
    f_leave(0)
    f_result(1)

    def jacobian(t, h, k):
        u = mixed[t, h, pl.ds(k * TILE, TILE)]
        r = inv_rms(u)
        unit = u * r
        g = br[t, h, k].astype(F32)
        back = r * (g - unit * jnp.mean(unit * g, axis=-1, keepdims=True))
        gm[k, :, pl.ds(pl.multiple_of(t * D + h * HD, HD), HD)] = back.astype(BF16)

    def b_queries(i, carry):
        h = ((x + ring_order(i // 2)) % 4) * 2 + i % 2
        landed(br.at[0, h], dq_rs.at[h])
        for k in range(2):
            jacobian(0, h, k)
        return carry

    lax.fori_loop(0, 8, b_queries, 0)

    def b_query_part(n, carry):
        cols = pl.ds(pl.multiple_of(n * 256, 256), 256)
        for k in range(2):
            gn[k, :, cols] = nn(gm[k, :, :D], wq[:D, cols])
        return carry

    lax.fori_loop(0, 4, b_query_part, 0)

    for k in range(2):
        for h in range(8):
            landed(br.at[pl.ds(1, 2), h, k], dkv_rs.at[k, h])
        if k == 1:
            f_leave(1)

        def b_keys(i, carry):
            for n in range(4):
                h = 4 * i + n
                jacobian(1, h, k)
                gm[k, :, pl.ds(pl.multiple_of(2 * D + h * HD, HD), HD)] = br[2, h, k]
            return carry

        lax.fori_loop(0, 2, b_keys, 0)

        def b_normed(n, carry):
            cols = pl.ds(pl.multiple_of(n * 512, 512), 512)
            gn[k, :, cols] += nn(gm[k, :, D:], wq[D:, cols])
            return carry

        lax.fori_loop(0, 2, b_normed, 0)
        rows = pl.ds(k * TILE, TILE)
        u = xin[1, rows].astype(F32)
        r = inv_rms(u)
        unit = u * r
        g = gn[k]
        back = r * (g - unit * jnp.mean(unit * g, axis=-1, keepdims=True))
        res[1, rows] = (xin[2, rows].astype(F32) + back).astype(BF16)

        @pl.when(z != 0)
        def _():
            pipe_start(1, k, og_hbm, (down, seq_of(x, b_source(k), y // 2)), y % 2, pb_ss, pb_rs)

    for j in range(2):
        exchange_sent(0, j, True)
        exchange_sent(1, j, False)
        exchange_sent(2, j, False)

    def drain(h, carry):
        @pl.when(h != b_me)
        def _():
            landed(sb.at[h, pl.ds(0, 3)], b_ss.at[h])
            landed(sb.at[h, 3], d_ss.at[h])
            landed(bo.at[0, h], dq_ss.at[h])
            for k in range(2):
                landed(bo.at[pl.ds(1, 2), h, k], dkv_ss.at[k, h])

        @pl.when(h != f_me)
        def _():
            landed(sf.at[h], f_ss.at[h])
            landed(fo.at[h], fo_ss.at[h])

        return carry

    lax.fori_loop(0, 8, drain, 0)

    @pl.when(z != 7)
    def _():
        for k in range(2):
            landed(res.at[0, pl.ds(k * TILE, TILE)], pf_ss.at[k])

    @pl.when(z != 0)
    def _():
        for k in range(2):
            landed(res.at[1, pl.ds(k * TILE, TILE)], pb_ss.at[k])
            landed(on_hbm.at[0, pl.ds(k * TILE, TILE)], pf_rs.at[k])

    @pl.when(z != 7)
    def _():
        for k in range(2):
            landed(og_hbm.at[0, pl.ds(k * TILE, TILE)], pb_rs.at[k])


def per_device(section_input, saved_input, grad_output, w_qkv, w_out, tile_cluster):
    any_spec = pl.BlockSpec(memory_space=pl.ANY)
    dma = pltpu.SemaphoreType.DMA
    block = jax.ShapeDtypeStruct((1, 2 * TILE, D), BF16)
    ahead, back = pl.pallas_call(
        kernel,
        out_shape=(block, block),
        in_specs=[pl.BlockSpec(memory_space=pltpu.SMEM)] + [any_spec] * 5,
        out_specs=(any_spec, any_spec),
        scratch_shapes=[
            pltpu.VMEM((3 * D, D), BF16),
            pltpu.VMEM((D, D), BF16),
            pltpu.VMEM((3, 2 * TILE, D), BF16),
            pltpu.VMEM((2, 2 * TILE, D), BF16),
            pltpu.VMEM((2, HEADS, 2 * TILE, HD), F32),
            pltpu.VMEM((HEADS, 3, 2, TILE, HD), BF16),
            pltpu.VMEM((HEADS, 4, 2, TILE, HD), BF16),
            pltpu.VMEM((3, GROUP + 1, TILE, HD), BF16),
            pltpu.VMEM((3, GROUP + 1, TILE, HD), BF16),
            pltpu.VMEM((GROUP + 1, TILE, HD), BF16),
            pltpu.VMEM((GROUP, TILE, CAP * TILE), F32),
            pltpu.VMEM((GROUP + 1, CAP, TILE, HD), BF16),
            pltpu.VMEM((GROUP + 1, CAP, TILE, HD), BF16),
            pltpu.VMEM((HEADS, 2, TILE, HD), BF16),
            pltpu.VMEM((HEADS, 2, TILE, HD), BF16),
            pltpu.VMEM((3, HEADS, 2, TILE, HD), BF16),
            pltpu.VMEM((3, HEADS, 2, TILE, HD), BF16),
            pltpu.VMEM((2 * TILE, D), BF16),
            pltpu.VMEM((2, TILE, 3 * D), BF16),
            pltpu.VMEM((2, TILE, D), F32),
            pltpu.VMEM((2, 2 * TILE, D), BF16),
            pltpu.SMEM((2 * GROUP * LIST,), jnp.int32),
            dma((2,)), dma((3, 2)), dma((3, 2)),
            dma((8,)), dma((8,)), dma((8,)), dma((8,)), dma((8,)), dma((8,)),
            dma((8,)), dma((8,)), dma((8,)), dma((8,)), dma((2, 8)), dma((2, 8)),
            dma((2,)), dma((2,)), dma((2,)), dma((2,)),
        ],
        compiler_params=pltpu.CompilerParams(
            collective_id=0, has_side_effects=True, vmem_limit_bytes=56 * 2**20
        ),
    )(tile_cluster, section_input, saved_input, grad_output, w_qkv, w_out)
    z = lax.axis_index("pipe")
    nothing = jnp.zeros((), BF16)
    return (
        jnp.where(z == 0, nothing, ahead),
        jnp.where(z == lax.axis_size("pipe") - 1, nothing, back),
    )


def solution(mesh):
    return jax.shard_map(
        per_device,
        mesh=mesh,
        in_specs=(
            P("pipe", "seq", None),
            P("pipe", "seq", None),
            P("pipe", "seq", None),
            P("pipe", None, None),
            P("pipe", None, None),
            P(),
        ),
        out_specs=(P("pipe", "seq", None), P("pipe", "seq", None)),
        check_vma=False,
    )
```

```python
import jax
import jax.numpy as jnp
from jax import lax
from jax.experimental import pallas as pl
from jax.experimental.pallas import tpu as pltpu
from jax.sharding import PartitionSpec as P

MESH = pl.DeviceIdType.MESH
HEADS = 8
HD = 128
TILE = 128
D = 1024
GROUP = 16
CAP = 3
LIST = 8
EPS = 1e-05
FACTOR = HD ** (-0.5)
F32 = jnp.float32
BF16 = jnp.bfloat16


def nt(a, b):
    return lax.dot_general(a, b, (((1,), (1,)), ((), ())), preferred_element_type=F32)


def tn(a, b):
    return lax.dot_general(a, b, (((0,), (0,)), ((), ())), preferred_element_type=F32)


def nn(a, b):
    return jnp.dot(a, b, preferred_element_type=F32)


def inv_rms(u):
    return lax.rsqrt(jnp.mean(u * u, axis=-1, keepdims=True) + EPS)


def ring_order(i):
    return (1 + 2 * i - 3 * (i // 2)) % 4


def landed(ref, sem):
    pltpu.make_async_copy(ref, ref, sem).wait()


def kernel(
    tc_ref, x_hbm, xs_hbm, g_hbm, wq_hbm, wo_hbm,
    on_hbm, og_hbm,
    wq, wo, xin, xn, mixed, sf, sb, rf, rb, rd, soft, dst, ptm, fo, fr, bo, br, att, gm, gn, res,
    lists,
    w_sem, ex_ss, ex_rs, f_ss, f_rs, b_ss, b_rs, d_ss, d_rs,
    fo_ss, fo_rs, dq_ss, dq_rs, dkv_ss, dkv_rs, pf_ss, pf_rs, pb_ss, pb_rs,
):
    z = lax.axis_index("pipe")
    s = lax.axis_index("seq")
    y = s // 8
    x = (s // 2) % 4
    c = s % 2

    def seq_of(xx, yy, cc):
        return (yy * 4 + xx) * 2 + cc

    def f_dev(h):
        return (z, seq_of(x, h // 2, h % 2))

    def b_dev(h):
        return (z, seq_of(h // 2, y, h % 2))

    f_me = y * 2 + c
    b_me = x * 2 + c
    up = (z + 1) % 8
    down = (z + 7) % 8

    w_copies = [
        pltpu.make_async_copy(wq_hbm.at[0], wq, w_sem.at[0]),
        pltpu.make_async_copy(wo_hbm.at[0], wo, w_sem.at[1]),
    ]
    for copy in w_copies:
        copy.start()

    barrier = pltpu.get_barrier_semaphore()

    def greet(dev):
        pl.semaphore_signal(barrier, inc=1, device_id=dev, device_id_type=MESH)

    for i in range(1, 8):
        greet(f_dev((f_me + i) % 8))
    for i in range(2, 8):
        greet(b_dev((2 * x + i) % 8))
    for k in range(2):
        for zz in (up, down):
            greet((zz, seq_of(2 * c + k, y, x // 2)))
            greet((zz, seq_of(x, 2 * c + k, y // 2)))
    pl.semaphore_wait(barrier, 21)

    def exchange(t, src_hbm, j, forward):
        other = 2 * c + j
        own = x if forward else y
        dev = (z, seq_of(other, y, x // 2) if forward else seq_of(x, other, y // 2))
        src = src_hbm.at[0, pl.ds(j * TILE, TILE)]
        slot = (own + j) % 2
        dst_ref = xin.at[t, pl.ds(slot * TILE, TILE)]
        recv = ex_rs.at[t, slot]

        @pl.when(own == other)
        def _():
            pltpu.make_async_copy(src, dst_ref, recv).start()

        @pl.when(own != other)
        def _():
            pltpu.make_async_remote_copy(
                src_ref=src, dst_ref=dst_ref, send_sem=ex_ss.at[t, j], recv_sem=recv,
                device_id=dev, device_id_type=MESH,
            ).start()

    def exchange_sent(t, j, forward):
        own = x if forward else y

        @pl.when(own != 2 * c + j)
        def _():
            landed(xin.at[t, pl.ds(j * TILE, TILE)], ex_ss.at[t, j])

    def exchange_wait(t):
        for k in range(2):
            landed(xin.at[t, pl.ds(k * TILE, TILE)], ex_rs.at[t, k])

    for j in range(2):
        exchange(1, xs_hbm, j, False)
        exchange(0, x_hbm, j, True)
    def f_source(k):
        return 2 * c + (k + x) % 2

    def b_source(k):
        return 2 * c + (k + y) % 2

    def fill(base, tile_of):
        ids = [tc_ref[tile_of(q)] for q in range(GROUP)]

        def one(q, carry):
            own_id = tc_ref[tile_of(q)]
            count = jnp.int32(0)
            rank = jnp.int32(0)
            members = [jnp.int32(GROUP)] * CAP
            for p in range(GROUP):
                same = ids[p] == own_id
                members = [
                    jnp.where(same & (count == k), p, members[k]) for k in range(CAP)
                ]
                rank = rank + jnp.where(same & (p < q), 1, 0)
                count = count + jnp.where(same, 1, 0)
            row = base + q * LIST
            for k in range(CAP):
                lists[row + k] = members[k]
            lists[row + 3] = jnp.minimum(rank, CAP - 1)
            lists[row + 4] = count
            return carry

        lax.fori_loop(0, GROUP, one, 0)

    fill(0, lambda q: 4 * ((q // 2) * 2 + (q + x) % 2) + x)
    fill(GROUP * LIST, lambda q: 4 * ((((q // 2) % 2) * 2 + (q + y) % 2) * 4 + q // 4) + y)

    zero = jnp.zeros((TILE, HD), BF16)
    for t in range(3):
        rf[t, GROUP] = zero
        rb[t, GROUP] = zero
    rd[GROUP] = zero
    for k in range(CAP):
        dst[GROUP, k] = zero
        ptm[GROUP, k] = zero

    def ship(src, dst_ref, send_sem, recv_sem, dev, is_self):
        @pl.when(is_self)
        def _():
            pltpu.make_async_copy(src, dst_ref, recv_sem).start()

        @pl.when(jnp.logical_not(is_self))
        def _():
            pltpu.make_async_remote_copy(
                src_ref=src, dst_ref=dst_ref, send_sem=send_sem, recv_sem=recv_sem,
                device_id=dev, device_id_type=MESH,
            ).start()

    def normalise(t, slot):
        for k in range(2):
            rows = pl.ds(k * TILE, TILE)
            u = xin[t, rows].astype(F32)
            xn[slot, rows] = (u * inv_rms(u)).astype(BF16)

    exchange_wait(1)
    for j in range(2):
        exchange(2, g_hbm, j, False)
    normalise(1, 1)
    w_copies[0].wait()

    def b_project(i, carry):
        a = (x + ring_order(i)) % 4
        rows = xn[1]
        for t in range(3):
            m = nt(rows, wq[pl.ds(pl.multiple_of(t * D + a * 256, 256), 256), :])
            for cc in range(2):
                u = m[:, cc * HD : (cc + 1) * HD]
                h = 2 * a + cc
                if t < 2:
                    mixed[t, h] = u
                    u = u * inv_rms(u)
                sb[h, t] = u.astype(BF16).reshape(2, TILE, HD)
        for cc in range(2):
            h = 2 * a + cc
            ship(
                sb.at[h, pl.ds(0, 3)], rb.at[:, pl.ds(2 * b_me, 2)],
                b_ss.at[h], b_rs.at[b_me], b_dev(h), h == b_me,
            )
        return carry

    lax.fori_loop(0, 4, b_project, 0)

    exchange_wait(0)
    normalise(0, 0)

    def f_project(i, carry):
        a = (y + ring_order(i)) % 4
        rows = xn[0]
        for t in range(3):
            m = nt(rows, wq[pl.ds(pl.multiple_of(t * D + a * 256, 256), 256), :])
            for cc in range(2):
                u = m[:, cc * HD : (cc + 1) * HD]
                if t < 2:
                    u = u * inv_rms(u)
                sf[2 * a + cc, t] = u.astype(BF16).reshape(2, TILE, HD)
        for cc in range(2):
            h = 2 * a + cc
            ship(
                sf.at[h], rf.at[:, pl.ds(2 * f_me, 2)],
                f_ss.at[h], f_rs.at[f_me], f_dev(h), h == f_me,
            )
        return carry

    lax.fori_loop(0, 4, f_project, 0)

    exchange_wait(2)
    w_copies[1].wait()

    def d_project(i, carry):
        a = (x + ring_order(i)) % 4
        m = nt(xin[2], wo[pl.ds(pl.multiple_of(a * 256, 256), 256), :])
        for cc in range(2):
            h = 2 * a + cc
            sb[h, 3] = m[:, cc * HD : (cc + 1) * HD].astype(BF16).reshape(2, TILE, HD)
            ship(
                sb.at[h, 3], rd.at[pl.ds(2 * b_me, 2)],
                d_ss.at[h], d_rs.at[b_me], b_dev(h), h == b_me,
            )
        return carry

    lax.fori_loop(0, 4, d_project, 0)

    def member_row(base, q):
        row = base + q * LIST
        return [lists[row + k] for k in range(5)]

    def weights_of(queries, keys, count):
        e = jnp.exp(nt(queries, keys) * FACTOR)
        parts = [e[:, :TILE]]
        for k in range(1, CAP):
            parts.append(e[:, k * TILE : (k + 1) * TILE] * jnp.where(count > k, 1.0, 0.0))
        total = jnp.sum(parts[0] + parts[1] + parts[2], axis=1, keepdims=True)
        return jnp.concatenate(parts, axis=1) * (1.0 / total)

    def stacked(ref, t, members):
        return jnp.concatenate([ref[t, m] for m in members], axis=0)

    for p in range(8):
        landed(rb.at[:, pl.ds(2 * p, 2)], b_rs.at[p])

    def b_soft(i, carry):
        for k in range(4):
            q = 4 * i + k
            m0, m1, m2, rank, count = member_row(GROUP * LIST, q)
            soft[q] = weights_of(rb[0, q], stacked(rb, 1, (m0, m1, m2)), count)
        return carry

    lax.fori_loop(0, 4, b_soft, 0)

    for p in range(8):
        landed(rd.at[pl.ds(2 * p, 2)], d_rs.at[p])

    def b_first(i, carry):
        a = (x + ring_order(i)) % 4
        for k in range(4):
            p = 2 * a + k // 2
            q = 4 * a + k
            m0, m1, m2, rank, count = member_row(GROUP * LIST, q)
            members = (m0, m1, m2)
            grad_soft = nt(rd[q], stacked(rb, 2, members))
            weights = soft[q]
            low = weights.astype(BF16)
            delta = jnp.sum(low.astype(F32) * grad_soft, axis=1, keepdims=True)
            grad_scores = (weights * (grad_soft - delta)).astype(BF16)
            for n in range(CAP):
                ptm[q, n] = low[:, n * TILE : (n + 1) * TILE]
                dst[q, n] = grad_scores[:, n * TILE : (n + 1) * TILE]
            bo[0, p, k % 2] = (nn(grad_scores, stacked(rb, 1, members)) * FACTOR).astype(BF16)
        for cc in range(2):
            p = 2 * a + cc
            ship(bo.at[0, p], br.at[0, b_me], dq_ss.at[p], dq_rs.at[b_me], b_dev(p), p == b_me)
        return carry

    lax.fori_loop(0, 4, b_first, 0)

    for p in range(8):
        landed(rf.at[:, pl.ds(2 * p, 2)], f_rs.at[p])

    def f_attend(i, carry):
        a = (y + ring_order(i)) % 4
        for k in range(4):
            q = 4 * a + k
            m0, m1, m2, rank, count = member_row(0, q)
            members = (m0, m1, m2)
            low = weights_of(rf[0, q], stacked(rf, 1, members), count).astype(BF16)
            fo[2 * a + k // 2, k % 2] = nn(low, stacked(rf, 2, members)).astype(BF16)
        for cc in range(2):
            p = 2 * a + cc
            ship(fo.at[p], fr.at[f_me], fo_ss.at[p], fo_rs.at[f_me], f_dev(p), p == f_me)
        return carry

    lax.fori_loop(0, 4, f_attend, 0)

    def b_second(i, carry):
        k = i // 4
        a = (x + ring_order(i % 4)) % 4
        for cc in range(2):
            p = 2 * a + cc
            q = 2 * p + k
            m0, m1, m2, rank, count = member_row(GROUP * LIST, q)
            members = (m0, m1, m2)
            ds = jnp.concatenate([dst[m, rank] for m in members], axis=0)
            pt = jnp.concatenate([ptm[m, rank] for m in members], axis=0)
            bo[1, p, k] = (tn(ds, stacked(rb, 0, members)) * FACTOR).astype(BF16)
            bo[2, p, k] = tn(pt, jnp.concatenate([rd[m] for m in members], axis=0)).astype(BF16)
        for cc in range(2):
            p = 2 * a + cc
            ship(
                bo.at[pl.ds(1, 2), p, k], br.at[pl.ds(1, 2), b_me, k],
                dkv_ss.at[k, p], dkv_rs.at[k, b_me], b_dev(p), p == b_me,
            )
        return carry

    lax.fori_loop(0, 8, b_second, 0)

    for h in range(HEADS):
        landed(fr.at[h], fo_rs.at[h])
        att[:, h * HD : (h + 1) * HD] = fr[h].reshape(2 * TILE, HD)

    def f_result(k):
        rows = pl.ds(k * TILE, TILE)

        def columns(n, carry):
            cols = pl.ds(pl.multiple_of(n * 512, 512), 512)
            total = xin[0, rows, cols].astype(F32) + nn(att[rows], wo[:, cols])
            res[0, rows, cols] = total.astype(BF16)
            return carry

        lax.fori_loop(0, 2, columns, 0)

    def pipe_start(result, k, out, dev, slot, send_sem, recv_sem):
        pltpu.make_async_remote_copy(
            src_ref=res.at[result, pl.ds(k * TILE, TILE)],
            dst_ref=out.at[0, pl.ds(slot * TILE, TILE)],
            send_sem=send_sem.at[k], recv_sem=recv_sem.at[slot],
            device_id=dev, device_id_type=MESH,
        ).start()

    def f_leave(k):
        @pl.when(z != 7)
        def _():
            pipe_start(0, k, on_hbm, (up, seq_of(f_source(k), y, x // 2)), x % 2, pf_ss, pf_rs)

    f_result(0)
    f_leave(0)
    f_result(1)

    def jacobian(t, h, k):
        u = mixed[t, h, pl.ds(k * TILE, TILE)]
        r = inv_rms(u)
        unit = u * r
        g = br[t, h, k].astype(F32)
        back = r * (g - unit * jnp.mean(unit * g, axis=-1, keepdims=True))
        gm[k, :, pl.ds(pl.multiple_of(t * D + h * HD, HD), HD)] = back.astype(BF16)

    for h in range(8):
        landed(br.at[0, h], dq_rs.at[h])

    def b_queries(i, carry):
        for n in range(2):
            for k in range(2):
                jacobian(0, 2 * i + n, k)
        return carry

    lax.fori_loop(0, 4, b_queries, 0)

    def b_query_part(n, carry):
        cols = pl.ds(pl.multiple_of(n * 512, 512), 512)
        for k in range(2):
            gn[k, :, cols] = nn(gm[k, :, :D], wq[:D, cols])
        return carry

    lax.fori_loop(0, 2, b_query_part, 0)

    for k in range(2):
        for h in range(8):
            landed(br.at[pl.ds(1, 2), h, k], dkv_rs.at[k, h])
        if k == 1:
            f_leave(1)

        def b_keys(i, carry):
            for n in range(4):
                h = 4 * i + n
                jacobian(1, h, k)
                gm[k, :, pl.ds(pl.multiple_of(2 * D + h * HD, HD), HD)] = br[2, h, k]
            return carry

        lax.fori_loop(0, 2, b_keys, 0)

        def b_normed(n, carry):
            cols = pl.ds(pl.multiple_of(n * 512, 512), 512)
            gn[k, :, cols] += nn(gm[k, :, D:], wq[D:, cols])
            return carry

        lax.fori_loop(0, 2, b_normed, 0)
        rows = pl.ds(k * TILE, TILE)
        u = xin[1, rows].astype(F32)
        r = inv_rms(u)
        unit = u * r
        g = gn[k]
        back = r * (g - unit * jnp.mean(unit * g, axis=-1, keepdims=True))
        res[1, rows] = (xin[2, rows].astype(F32) + back).astype(BF16)

        @pl.when(z != 0)
        def _():
            pipe_start(1, k, og_hbm, (down, seq_of(x, b_source(k), y // 2)), y % 2, pb_ss, pb_rs)

    for j in range(2):
        exchange_sent(0, j, True)
        exchange_sent(1, j, False)
        exchange_sent(2, j, False)

    def drain(h, carry):
        @pl.when(h != b_me)
        def _():
            landed(sb.at[h, pl.ds(0, 3)], b_ss.at[h])
            landed(sb.at[h, 3], d_ss.at[h])
            landed(bo.at[0, h], dq_ss.at[h])
            for k in range(2):
                landed(bo.at[pl.ds(1, 2), h, k], dkv_ss.at[k, h])

        @pl.when(h != f_me)
        def _():
            landed(sf.at[h], f_ss.at[h])
            landed(fo.at[h], fo_ss.at[h])

        return carry

    lax.fori_loop(0, 8, drain, 0)

    @pl.when(z != 7)
    def _():
        for k in range(2):
            landed(res.at[0, pl.ds(k * TILE, TILE)], pf_ss.at[k])

    @pl.when(z != 0)
    def _():
        for k in range(2):
            landed(res.at[1, pl.ds(k * TILE, TILE)], pb_ss.at[k])
            landed(on_hbm.at[0, pl.ds(k * TILE, TILE)], pf_rs.at[k])

    @pl.when(z != 7)
    def _():
        for k in range(2):
            landed(og_hbm.at[0, pl.ds(k * TILE, TILE)], pb_rs.at[k])


def per_device(section_input, saved_input, grad_output, w_qkv, w_out, tile_cluster):
    any_spec = pl.BlockSpec(memory_space=pl.ANY)
    dma = pltpu.SemaphoreType.DMA
    block = jax.ShapeDtypeStruct((1, 2 * TILE, D), BF16)
    ahead, back = pl.pallas_call(
        kernel,
        out_shape=(block, block),
        in_specs=[pl.BlockSpec(memory_space=pltpu.SMEM)] + [any_spec] * 5,
        out_specs=(any_spec, any_spec),
        scratch_shapes=[
            pltpu.VMEM((3 * D, D), BF16),
            pltpu.VMEM((D, D), BF16),
            pltpu.VMEM((3, 2 * TILE, D), BF16),
            pltpu.VMEM((2, 2 * TILE, D), BF16),
            pltpu.VMEM((2, HEADS, 2 * TILE, HD), F32),
            pltpu.VMEM((HEADS, 3, 2, TILE, HD), BF16),
            pltpu.VMEM((HEADS, 4, 2, TILE, HD), BF16),
            pltpu.VMEM((3, GROUP + 1, TILE, HD), BF16),
            pltpu.VMEM((3, GROUP + 1, TILE, HD), BF16),
            pltpu.VMEM((GROUP + 1, TILE, HD), BF16),
            pltpu.VMEM((GROUP, TILE, CAP * TILE), F32),
            pltpu.VMEM((GROUP + 1, CAP, TILE, HD), BF16),
            pltpu.VMEM((GROUP + 1, CAP, TILE, HD), BF16),
            pltpu.VMEM((HEADS, 2, TILE, HD), BF16),
            pltpu.VMEM((HEADS, 2, TILE, HD), BF16),
            pltpu.VMEM((3, HEADS, 2, TILE, HD), BF16),
            pltpu.VMEM((3, HEADS, 2, TILE, HD), BF16),
            pltpu.VMEM((2 * TILE, D), BF16),
            pltpu.VMEM((2, TILE, 3 * D), BF16),
            pltpu.VMEM((2, TILE, D), F32),
            pltpu.VMEM((2, 2 * TILE, D), BF16),
            pltpu.SMEM((2 * GROUP * LIST,), jnp.int32),
            dma((2,)), dma((3, 2)), dma((3, 2)),
            dma((8,)), dma((8,)), dma((8,)), dma((8,)), dma((8,)), dma((8,)),
            dma((8,)), dma((8,)), dma((8,)), dma((8,)), dma((2, 8)), dma((2, 8)),
            dma((2,)), dma((2,)), dma((2,)), dma((2,)),
        ],
        compiler_params=pltpu.CompilerParams(
            collective_id=0, has_side_effects=True, vmem_limit_bytes=56 * 2**20
        ),
    )(tile_cluster, section_input, saved_input, grad_output, w_qkv, w_out)
    z = lax.axis_index("pipe")
    nothing = jnp.zeros((), BF16)
    return (
        jnp.where(z == 0, nothing, ahead),
        jnp.where(z == lax.axis_size("pipe") - 1, nothing, back),
    )


def solution(mesh):
    return jax.shard_map(
        per_device,
        mesh=mesh,
        in_specs=(
            P("pipe", "seq", None),
            P("pipe", "seq", None),
            P("pipe", "seq", None),
            P("pipe", None, None),
            P("pipe", None, None),
            P(),
        ),
        out_specs=(P("pipe", "seq", None), P("pipe", "seq", None)),
        check_vma=False,
    )
```
